32 devices in a mesh: tm: 4 (over y, core), rows: 8 (over z, x).
Axes of the slice: x: 2, y: 2, z: 4, core: 2. Of those that a mesh axis runs over, the one named last changes fastest.
Arguments:
- features: bfloat16 [16, 16, 320, 128], P('tm', 'rows'), may hold values from -20 to 20
- gain_one: float32 [128], replicated, may hold values from 0.1 to 1.9
- shift_one: float32 [128], replicated, may hold values from -4 to 4
- weight_one: bfloat16 [3456, 128], replicated, may hold values from -0.109375 to 0.109375
- bias_one: float32 [128], replicated, may hold values from -6 to 6
- gain_two: float32 [128], replicated, may hold values from 0.1 to 1.9
- shift_two: float32 [128], replicated, may hold values from -4 to 4
- weight_two: bfloat16 [3456, 128], replicated, may hold values from -0.109375 to 0.109375
- bias_two: float32 [128], replicated, may hold values from -6 to 6
Outputs:
- block_out: bfloat16 [16, 16, 320, 128], P('tm', 'rows')
The draws below stay inside these ranges and needn't reach their ends.
All inputs are finite; a program needn't handle non-finite values.
Results may differ from the reference program's by a relative error of at most 0.007.
Values may be sent and summed in bfloat16 or wider, within the bound.
A program may use at most 64 MiB of HBM per device.

```python
import jax
import jax.numpy as jnp
from jax import lax

C = 128
GROUPS = 32
W = 320
NT = 16
H = 16


def draw_features(key, part):
    base_key = jax.random.fold_in(key, 17)
    noise_key, mean_key = jax.random.split(base_key, 2)
    frame_pos = jnp.arange(NT, dtype=jnp.float32) / max(NT - 1, 1)
    row_pos = jnp.arange(H, dtype=jnp.float32) / max(H - 1, 1)
    rising = 0.6 * (1.0 + frame_pos[:, None] + row_pos[None, :])
    offsets = jax.random.uniform(mean_key, (C,), jnp.float32, -0.6, 0.6)
    noise = jnp.clip(jax.random.normal(noise_key, (NT, H, W, C), jnp.float32), -4.0, 4.0)
    values = (noise + offsets) * rising[:, :, None, None]
    return values.astype(jnp.bfloat16)


def gaussian(own_key, extent, scale, most, held_as=jnp.bfloat16):
    array = scale * jax.random.normal(own_key, extent, jnp.float32)
    return jnp.clip(array, min=-most, max=most).astype(held_as)


def setup_inputs(seed: int = 0) -> dict:
    keys = jax.random.split(jax.random.key(seed), 10)
    return {
        "features": draw_features(jax.random.fold_in(keys[9], 71), 0),
        "gain_one": jnp.clip(1.0 + 0.18 * jax.random.normal(keys[1], (C,), jnp.float32), 0.1, 1.9),
        "shift_one": gaussian(keys[2], (C,), 0.3, 4.0, jnp.float32),
        "weight_one": gaussian(keys[3], (27 * C, C), (27 * C) ** -0.5, 0.109375),
        "bias_one": gaussian(keys[4], (C,), 0.5, 6.0, jnp.float32),
        "gain_two": jnp.clip(1.0 + 0.18 * jax.random.normal(keys[5], (C,), jnp.float32), 0.1, 1.9),
        "shift_two": gaussian(keys[6], (C,), 0.3, 4.0, jnp.float32),
        "weight_two": gaussian(keys[7], (27 * C, C), (27 * C) ** -0.5, 0.109375),
        "bias_two": gaussian(keys[8], (C,), 0.5, 6.0, jnp.float32),
    }


EPS = 1e-06

def group_moments(values):
    cell_count = values.shape[0] * values.shape[1] * values.shape[2] * (C // GROUPS)
    per_channel = lax.optimization_barrier(jnp.sum(values, axis=(0, 1, 2)))
    average = lax.optimization_barrier(jnp.sum(per_channel.reshape(GROUPS, -1), axis=1)) / cell_count
    centered = values - jnp.repeat(average, C // GROUPS)
    squares = lax.optimization_barrier(jnp.sum(centered * centered, axis=(0, 1, 2)))
    spread = lax.optimization_barrier(jnp.sum(squares.reshape(GROUPS, -1), axis=1)) / cell_count
    return (average, spread)

def activate(values, average, spread, gain, shift):
    center = jnp.repeat(average, C // GROUPS)
    factor = jnp.repeat(lax.rsqrt(spread + EPS), C // GROUPS)
    normed = (values - center) * factor * gain + shift
    return jax.nn.silu(normed).astype(jnp.bfloat16)

def causal_conv(activated, weight, bias):
    padded = jnp.concatenate([activated[:1], activated[:1], activated], 0)
    padded = jnp.pad(padded, ((0, 0), (1, 1), (1, 1), (0, 0)))

    def one_frame(frame):
        window = lax.dynamic_slice_in_dim(padded, frame, 3, 0)
        summed = jnp.zeros((H * W, C), jnp.float32)
        for time_tap in range(3):
            for row_tap in range(3):
                columns = jnp.concatenate([window[time_tap, row_tap:row_tap + H, col_tap:col_tap + W] for col_tap in range(3)], -1)
                first_row = (time_tap * 3 + row_tap) * 3 * C
                taps_block = weight[first_row:first_row + 3 * C]
                summed = summed + jnp.dot(columns.reshape(H * W, 3 * C), taps_block, preferred_element_type=jnp.float32)
        return summed.reshape(H, W, C) + bias
    return lax.map(one_frame, jnp.arange(NT, dtype=jnp.int32))

def reference(features, gain_one, shift_one, weight_one, bias_one, gain_two, shift_two, weight_two, bias_two):
    inputs = features.astype(jnp.float32)
    average, spread = group_moments(inputs)
    activated = activate(inputs, average, spread, gain_one, shift_one)
    hidden = causal_conv(activated, weight_one, bias_one).astype(jnp.bfloat16)
    hidden_wide = hidden.astype(jnp.float32)
    average_two, spread_two = group_moments(hidden_wide)
    second = activate(hidden_wide, average_two, spread_two, gain_two, shift_two)
    result = causal_conv(second, weight_two, bias_two) + inputs
    return result.astype(jnp.bfloat16)
```

```python
import functools

import jax
import jax.numpy as jnp
from jax import lax
from jax.experimental import pallas as pl
from jax.experimental.pallas import tpu as pltpu
from jax.sharding import PartitionSpec as P

GROUPS = 32
EPS = 1e-06
LEAD = 2
STAT_ROWS = 8


def group_total(values, size):
    lanes = values.shape[-1]
    lane = lax.broadcasted_iota(jnp.int32, values.shape, 1)
    step = 1
    while step < size:
        left = pltpu.roll(values, step, 1)
        right = pltpu.roll(values, lanes - step, 1)
        values = values + jnp.where((lane & step) == 0, right, left)
        step *= 2
    return values


def kernel(
    tm_count, row_count,
    x_ref, gain1_ref, shift1_ref, w1_ref, bias1_ref, gain2_ref, shift2_ref, w2_ref, bias2_ref,
    out_ref,
    act, big1, big2, hid, up, dn, pre, mine, stat_a, stat_b,
    w_sem, send_sem, recv_sem, sa_send, sa_recv, sb_send, sb_recv,
):
    frames, rows, width, chans = x_ref.shape
    tm = lax.axis_index("tm")
    row = lax.axis_index("rows")
    has_up = row > 0
    has_dn = row < row_count - 1
    has_prev = tm > 0
    has_next = tm < tm_count - 1
    span = 3 * chans
    depth = 3 * span
    size = chans // GROUPS
    total = float(frames * rows * width * size * tm_count * row_count)

    def weight_copies(which, src, dst):
        return [
            pltpu.make_async_copy(
                src.at[pl.ds(i * depth, depth)],
                dst.at[i, pl.ds(o * span, depth), pl.ds(o * chans, chans)],
                w_sem.at[which, i * rows + o],
            )
            for i in range(3)
            for o in range(rows)
        ]

    loads1 = weight_copies(0, w1_ref, big1)
    loads2 = weight_copies(1, w2_ref, big2)
    for copy in loads1 + loads2:
        copy.start()

    barrier = pltpu.get_barrier_semaphore()
    for k in range(1, row_count):
        pl.semaphore_signal(barrier, inc=1, device_id={"rows": lax.rem(row + k, row_count)})
    for k in range(1, tm_count):
        pl.semaphore_signal(barrier, inc=1, device_id={"tm": lax.rem(tm + k, tm_count)})
    pl.semaphore_wait(barrier, row_count + tm_count - 2)

    def halo(phase, src):
        early, late = frames - LEAD, LEAD
        below = {"rows": jnp.minimum(row + 1, row_count - 1)}
        above = {"rows": jnp.maximum(row - 1, 0)}
        after = {"tm": jnp.minimum(tm + 1, tm_count - 1)}

        def copy(n, source, target, device):
            return pltpu.make_async_remote_copy(
                src_ref=source, dst_ref=target,
                send_sem=send_sem.at[phase, n], recv_sem=recv_sem.at[phase, n],
                device_id=device,
            )

        u, d, p = up.at[phase], dn.at[phase], pre.at[phase]
        return {
            "down_late": copy(0, src.at[pl.ds(early, late), rows - 1], u.at[pl.ds(LEAD + early, late)], below),
            "up_late": copy(1, src.at[pl.ds(early, late), 0], d.at[pl.ds(LEAD + early, late)], above),
            "down_early": copy(2, src.at[pl.ds(0, early), rows - 1], u.at[pl.ds(LEAD, early)], below),
            "up_early": copy(3, src.at[pl.ds(0, early), 0], d.at[pl.ds(LEAD, early)], above),
            "next": copy(4, src.at[pl.ds(early, late)], p, after),
            "corner_up": copy(5, u.at[pl.ds(LEAD + early, late)], u.at[pl.ds(0, LEAD)], after),
            "corner_dn": copy(6, d.at[pl.ds(LEAD + early, late)], d.at[pl.ds(0, LEAD)], after),
        }

    def when(cond, fn):
        pl.when(cond)(fn)

    def send_late(c):
        when(has_dn, c["down_late"].start)
        when(has_up, c["up_late"].start)
        when(has_next, c["next"].start)

    def send_early(c):
        when(has_dn, c["down_early"].start)
        when(has_up, c["up_early"].start)

    def forward(c):
        @pl.when(has_up)
        def _():
            c["down_late"].wait_recv()
            when(has_next, c["corner_up"].start)

        @pl.when(has_dn)
        def _():
            c["up_late"].wait_recv()
            when(has_next, c["corner_dn"].start)

    def finish_sends(c):
        @pl.when(has_dn)
        def _():
            c["down_late"].wait_send()
            c["down_early"].wait_send()
            when(has_next, c["corner_dn"].wait_send)

        @pl.when(has_up)
        def _():
            c["up_late"].wait_send()
            c["up_early"].wait_send()
            when(has_next, c["corner_up"].wait_send)

        when(has_next, c["next"].wait_send)

    def reduce_stats(phase, src):
        first = jnp.zeros((8, chans), jnp.float32)
        square = jnp.zeros((8, chans), jnp.float32)

        def add(n, carry):
            s, q = carry
            v = src[n // rows, n % rows].astype(jnp.float32).reshape(width // 8, 8, chans)
            return s + jnp.sum(v, axis=0), q + jnp.sum(v * v, axis=0)

        first, square = lax.fori_loop(0, frames * rows, add, (first, square))
        part = jnp.concatenate(
            [
                jnp.sum(first, axis=0, keepdims=True),
                jnp.sum(square, axis=0, keepdims=True),
                jnp.zeros((STAT_ROWS - 2, chans), jnp.float32),
            ],
            axis=0,
        )
        for axis, me, count, slots, send, recv in (
            ("rows", row, row_count, stat_a, sa_send, sa_recv),
            ("tm", tm, tm_count, stat_b, sb_send, sb_recv),
        ):
            slots[phase, 0] = part
            copies = []
            for k in range(1, count):
                copy = pltpu.make_async_remote_copy(
                    src_ref=slots.at[phase, 0], dst_ref=slots.at[phase, k],
                    send_sem=send.at[phase, k], recv_sem=recv.at[phase, k],
                    device_id={axis: lax.rem(me + k, count)},
                )
                copy.start()
                copies.append(copy)
            for copy in copies:
                copy.wait_recv()
            part = jnp.sum(slots[phase], axis=0)
            for copy in copies:
                copy.wait_send()
        mean = group_total(part, size) / total
        average = mean[0:1]
        spread = mean[1:2] - average * average
        return average, spread

    def coefficients(stats, gain_ref, shift_ref):
        average, spread = stats
        factor = lax.rsqrt(spread + EPS) * gain_ref[...] * 0.5
        return average, factor, shift_ref[...] * 0.5

    edge = lax.broadcasted_iota(jnp.int32, (width, chans), 0)

    def activate(cell, coef, frame, place):
        average, factor, offset = coef
        half = (cell.astype(jnp.float32) - average) * factor + offset
        value = half + half * jnp.tanh(half)
        left = jnp.where(edge == 0, 0.0, pltpu.roll(value, 1, 0))
        right = jnp.where(edge == width - 1, 0.0, pltpu.roll(value, width - 1, 0))
        base = place * span
        act[frame, :, pl.ds(base, chans)] = left.astype(jnp.bfloat16)
        act[frame, :, pl.ds(base + chans, chans)] = value.astype(jnp.bfloat16)
        act[frame, :, pl.ds(base + 2 * chans, chans)] = right.astype(jnp.bfloat16)

    def activate_own(src, coef):
        for r in range(rows):
            @pl.loop(0, frames)
            def _(f):
                activate(src[f, r], coef, f + LEAD, r + 1)

    def activate_side(buf, coef, place, first, count):
        @pl.loop(first, first + count)
        def _(f):
            activate(buf[f], coef, f, place)

    def halos(phase, c, coef):
        @pl.when(has_prev)
        def _():
            c["next"].wait_recv()
            for r in range(rows):
                @pl.loop(0, LEAD)
                def _(f):
                    activate(pre[phase, f, r], coef, f, r + 1)

        for cond, buf, place, late, early, corner in (
            (has_up, up.at[phase], 0, "down_late", "down_early", "corner_up"),
            (has_dn, dn.at[phase], rows + 1, "up_late", "up_early", "corner_dn"),
        ):
            @pl.when(cond)
            def _():
                activate_side(buf, coef, place, frames, LEAD)
                c[early].wait_recv()
                activate_side(buf, coef, place, LEAD, frames - LEAD)

                @pl.when(has_prev)
                def _():
                    c[corner].wait_recv()
                    activate_side(buf, coef, place, 0, LEAD)

        @pl.when(jnp.logical_not(has_prev))
        def _():
            for f in range(LEAD):
                act[f] = act[LEAD]

    def conv(frame, big, bias_ref):
        summed = jnp.dot(act[frame], big[0], preferred_element_type=jnp.float32)
        for i in range(1, 3):
            summed = summed + jnp.dot(act[frame + i], big[i], preferred_element_type=jnp.float32)
        return [summed[:, o * chans : (o + 1) * chans] + bias_ref[...] for o in range(rows)]

    ahead = halo(0, x_ref)
    send_late(ahead)
    send_early(ahead)

    for big in (big1, big2):
        for i in range(3):
            for o in range(rows):
                cols = pl.ds(o * chans, chans)
                if o > 0:
                    big[i, pl.ds(0, o * span), cols] = jnp.zeros((o * span, chans), jnp.bfloat16)
                rest = (rows - 1 - o) * span
                if rest > 0:
                    big[i, pl.ds(o * span + depth, rest), cols] = jnp.zeros((rest, chans), jnp.bfloat16)

    for cond, place in ((has_up, 0), (has_dn, rows + 1)):
        @pl.when(jnp.logical_not(cond))
        def _():
            for f in range(frames + LEAD):
                act[f, :, pl.ds(place * span, span)] = jnp.zeros((width, span), jnp.bfloat16)

    coef = coefficients(reduce_stats(0, x_ref), gain1_ref, shift1_ref)
    activate_own(x_ref, coef)
    forward(ahead)
    halos(0, ahead, coef)
    for copy in loads1:
        copy.wait()

    behind = halo(1, hid)

    def first_conv(f):
        for r, value in enumerate(conv(f, big1, bias1_ref)):
            hid[f, r] = value.astype(jnp.bfloat16)

    @pl.loop(frames - LEAD, frames)
    def _(f):
        first_conv(f)

    send_late(behind)

    @pl.loop(0, frames - LEAD)
    def _(f):
        first_conv(f)

    send_early(behind)
    coef = coefficients(reduce_stats(1, hid), gain2_ref, shift2_ref)
    activate_own(hid, coef)
    forward(behind)
    halos(1, behind, coef)
    for copy in loads2:
        copy.wait()

    @pl.loop(0, frames)
    def _(f):
        for r, value in enumerate(conv(f, big2, bias2_ref)):
            out_ref[f, r] = (value + x_ref[f, r].astype(jnp.float32)).astype(jnp.bfloat16)

    finish_sends(ahead)
    finish_sends(behind)


def body(tm_count, row_count, features, gain1, shift1, w1, bias1, gain2, shift2, w2, bias2):
    frames, rows, width, chans = features.shape
    lanes = (rows + 2) * 3 * chans
    vmem = pl.BlockSpec(memory_space=pltpu.VMEM)
    hbm = pl.BlockSpec(memory_space=pl.ANY)
    bf16, f32 = jnp.bfloat16, jnp.float32
    dma = pltpu.SemaphoreType.DMA
    return pl.pallas_call(
        functools.partial(kernel, tm_count, row_count),
        out_shape=jax.ShapeDtypeStruct(features.shape, bf16),
        in_specs=[vmem, vmem, vmem, hbm, vmem, vmem, vmem, hbm, vmem],
        out_specs=vmem,
        scratch_shapes=[
            pltpu.VMEM((frames + LEAD, width, lanes), bf16),
            pltpu.VMEM((3, lanes, rows * chans), bf16),
            pltpu.VMEM((3, lanes, rows * chans), bf16),
            pltpu.VMEM((frames, rows, width, chans), bf16),
            pltpu.VMEM((2, frames + LEAD, width, chans), bf16),
            pltpu.VMEM((2, frames + LEAD, width, chans), bf16),
            pltpu.VMEM((2, LEAD, rows, width, chans), bf16),
            pltpu.VMEM((STAT_ROWS, chans), f32),
            pltpu.VMEM((2, row_count, STAT_ROWS, chans), f32),
            pltpu.VMEM((2, tm_count, STAT_ROWS, chans), f32),
            dma((2, 3 * rows)),
            dma((2, 7)),
            dma((2, 7)),
            dma((2, row_count)),
            dma((2, row_count)),
            dma((2, tm_count)),
            dma((2, tm_count)),
        ],
        compiler_params=pltpu.CompilerParams(
            collective_id=0, has_side_effects=True, vmem_limit_bytes=40 * 1024 * 1024
        ),
        name="block",
    )(
        features, gain1.reshape(1, -1), shift1.reshape(1, -1), w1, bias1.reshape(1, -1),
        gain2.reshape(1, -1), shift2.reshape(1, -1), w2, bias2.reshape(1, -1),
    )


def solution(mesh):
    in_specs = (P("tm", "rows", None, None), P(), P(), P(), P(), P(), P(), P(), P())
    out_specs = P("tm", "rows", None, None)
    return jax.shard_map(
        functools.partial(body, mesh.shape["tm"], mesh.shape["rows"]),
        mesh=mesh, in_specs=in_specs, out_specs=out_specs, check_vma=False,
    )
```

```python
import functools

import jax
import jax.numpy as jnp
from jax import lax
from jax.experimental import pallas as pl
from jax.experimental.pallas import tpu as pltpu
from jax.sharding import PartitionSpec as P

GROUPS = 32
EPS = 1e-06
LEAD = 2
STAT_ROWS = 8


def group_total(values, size):
    lanes = values.shape[-1]
    lane = lax.broadcasted_iota(jnp.int32, values.shape, 1)
    step = 1
    while step < size:
        left = pltpu.roll(values, step, 1)
        right = pltpu.roll(values, lanes - step, 1)
        values = values + jnp.where((lane & step) == 0, right, left)
        step *= 2
    return values


def kernel(
    tm_count, row_count,
    x_hbm, gain1_hbm, shift1_hbm, w1_ref, bias1_hbm, gain2_hbm, shift2_hbm, w2_ref, bias2_hbm,
    out_hbm,
    x_ref, raw, hid, act, big1, big2, stage, out_buf, small, stat_a, stat_b,
    load_sem, w_sem, send_sem, recv_sem, sa_send, sa_recv, sb_send, sb_recv, store_sem,
):
    frames, rows, width, chans = x_ref.shape
    window = raw.shape[2]
    half = width // 2
    pad = window - half
    tall = 2 * rows
    early, late = frames - LEAD, LEAD
    tm = lax.axis_index("tm")
    row = lax.axis_index("rows")
    side = lax.rem(row, 2)
    pair = row // 2
    partner = {"rows": row + 1 - 2 * side}
    has_up = pair > 0
    has_dn = pair < row_count // 2 - 1
    has_prev = tm > 0
    has_next = tm < tm_count - 1
    left_side = side == 0
    above_row = jnp.maximum(row - 2, side)
    below_row = jnp.minimum(row + 2, row_count - 2 + side)
    above, below = {"rows": above_row}, {"rows": below_row}
    above_across = {"rows": above_row + 1 - 2 * side}
    below_across = {"rows": below_row + 1 - 2 * side}
    after = {"tm": jnp.minimum(tm + 1, tm_count - 1)}
    span = 3 * chans
    depth = 3 * span
    size = chans // GROUPS
    total = float(frames * rows * width * size * tm_count * row_count)

    def aligned(value):
        return pl.multiple_of(value, 16)

    mine = pl.ds(aligned(side * (half - pad)), window)
    theirs = pl.ds(aligned((1 - side) * (half - pad)), window)
    own_rows = pl.ds(1 + side * rows, rows)
    own_cols = pl.ds(aligned(side * pad), half)
    edge_src = pl.ds(aligned(half - pad - side * (half - 2 * pad)), pad)
    edge_dst = pl.ds(aligned(side * half), pad)
    half_cols = pl.ds(aligned(side * half), half)

    def weight_copies(which, src, dst):
        return [
            pltpu.make_async_copy(
                src.at[pl.ds(i * depth, depth)],
                dst.at[i, pl.ds(o * span, depth), pl.ds(o * chans, chans)],
                w_sem.at[which, i * rows + o],
            )
            for i in range(3)
            for o in range(rows)
        ]

    load_x = pltpu.make_async_copy(x_hbm, x_ref, load_sem.at[0])
    load_raw = pltpu.make_async_copy(
        x_hbm.at[:, :, mine], raw.at[pl.ds(LEAD, frames), own_rows], load_sem.at[1]
    )
    load_small = [
        pltpu.make_async_copy(src, small.at[n], load_sem.at[2 + n])
        for n, src in enumerate((gain1_hbm, shift1_hbm, bias1_hbm, gain2_hbm, shift2_hbm, bias2_hbm))
    ]
    loads1 = weight_copies(0, w1_ref, big1)
    loads2 = weight_copies(1, w2_ref, big2)
    for copy in [load_x, load_raw] + load_small + loads1 + loads2:
        copy.start()

    barrier = pltpu.get_barrier_semaphore()
    for k in range(1, row_count):
        pl.semaphore_signal(barrier, inc=1, device_id={"rows": lax.rem(row + k, row_count)})
    for k in range(1, tm_count):
        pl.semaphore_signal(barrier, inc=1, device_id={"tm": lax.rem(tm + k, tm_count)})

    used = [0]

    def remote(source, target, device):
        n = used[0]
        used[0] += 1
        return pltpu.make_async_remote_copy(
            src_ref=source, dst_ref=target, send_sem=send_sem.at[n], recv_sem=recv_sem.at[n],
            device_id=device,
        )

    parts = (pl.ds(LEAD + early, late), pl.ds(LEAD, early))
    source_parts = (pl.ds(early, late), pl.ds(0, early))

    swap = [
        remote(x_hbm.at[s, :, theirs], raw.at[d, own_rows], partner)
        for s, d in zip(source_parts, parts)
    ]

    def halo_copies(buf, cols):
        ups = [remote(buf.at[d, 1, cols], buf.at[d, tall + 1, cols], above) for d in parts]
        dns = [remote(buf.at[d, tall, cols], buf.at[d, 0, cols], below) for d in parts]
        first = pl.ds(0, LEAD)
        nexts = [
            remote(buf.at[parts[0], r], buf.at[first, r], after)
            for r in (pl.ds(1, tall), 0, tall + 1)
        ]
        return ups, dns, nexts

    ups1, dns1, nexts1 = halo_copies(raw, pl.ds(0, window))
    ups2, dns2, nexts2 = halo_copies(hid, own_cols)
    across = [
        remote(hid.at[d, pl.ds(1, tall), edge_src], hid.at[d, pl.ds(1, tall), edge_dst], partner)
        for d in parts
    ]
    ups_across = [
        remote(hid.at[d, 1, edge_src], hid.at[d, tall + 1, edge_dst], above_across) for d in parts
    ]
    dns_across = [
        remote(hid.at[d, tall, edge_src], hid.at[d, 0, edge_dst], below_across) for d in parts
    ]
    gives = [
        remote(stage.at[f], out_buf.at[f, :, half_cols], partner) for f in range(frames)
    ]

    def when(cond, fn):
        pl.when(cond)(fn)

    def local_stats(cells):
        def add(n, carry):
            s, q = carry
            v = cells(n).astype(jnp.float32)
            v = v.reshape(v.shape[0] // 8, 8, chans)
            return s + jnp.sum(v, axis=0), q + jnp.sum(v * v, axis=0)

        zero = jnp.zeros((8, chans), jnp.float32)
        return zero, add

    def summed_part(count, cells):
        zero, add = local_stats(cells)
        first, square = lax.fori_loop(0, count, add, (zero, zero))
        return jnp.concatenate(
            [
                jnp.sum(first, axis=0, keepdims=True),
                jnp.sum(square, axis=0, keepdims=True),
                jnp.zeros((STAT_ROWS - 2, chans), jnp.float32),
            ],
            axis=0,
        )

    def send_stats(phase, part, axis, me, count, slots, send, recv):
        slots[phase, 0] = part
        copies = []
        for k in range(1, count):
            copy = pltpu.make_async_remote_copy(
                src_ref=slots.at[phase, 0], dst_ref=slots.at[phase, k],
                send_sem=send.at[phase, k], recv_sem=recv.at[phase, k],
                device_id={axis: lax.rem(me + k, count)},
            )
            copy.start()
            copies.append(copy)
        return copies

    def stats_rows(phase, part):
        return send_stats(phase, part, "rows", row, row_count, stat_a, sa_send, sa_recv)

    def stats_tm(phase, part):
        return send_stats(phase, part, "tm", tm, tm_count, stat_b, sb_send, sb_recv)

    def collect(phase, copies, slots):
        for copy in copies:
            copy.wait_recv()
        return jnp.sum(slots[phase], axis=0)

    def coefficients(part, gain, shift):
        mean = group_total(part, size) / total
        average = mean[0:1]
        spread = mean[1:2] - average * average
        return average, lax.rsqrt(spread + EPS) * gain * 0.5, shift * 0.5

    edge = lax.broadcasted_iota(jnp.int32, (window, chans), 0)

    def activate(cell, coef, frame, place):
        average, factor, offset = coef
        h = (cell.astype(jnp.float32) - average) * factor + offset
        value = h + h * jnp.tanh(h)
        left = jnp.where(edge == 0, 0.0, pltpu.roll(value, 1, 0))
        right = jnp.where(edge == window - 1, 0.0, pltpu.roll(value, window - 1, 0))
        base = pl.multiple_of(place * span, chans)
        act[frame, :, pl.ds(base, chans)] = left.astype(jnp.bfloat16)
        act[frame, :, pl.ds(base + chans, chans)] = value.astype(jnp.bfloat16)
        act[frame, :, pl.ds(base + 2 * chans, chans)] = right.astype(jnp.bfloat16)

    def activate_block(buf, coef, first, count, top, height):
        @pl.loop(0, count * height)
        def _(n):
            f, r = first + n // height, top + n % height
            activate(buf[f, r], coef, f, r)

    def activate_edges(buf, coef, ups, dns, ups_more, dns_more, nexts, part):
        first, count = ((LEAD + early, late), (LEAD, early))[part]
        for cond, copies, more, place in (
            (has_up, dns, dns_more, 0), (has_dn, ups, ups_more, tall + 1)
        ):
            @pl.when(cond)
            def _():
                if part == 1:
                    copies[part].wait_recv()
                    if more:
                        more[part].wait_recv()
                activate_block(buf, coef, first, count, place, 1)

    def activate_lead(buf, coef, nexts):
        @pl.when(has_prev)
        def _():
            nexts[0].wait_recv()
            activate_block(buf, coef, 0, LEAD, 1, tall)
            for cond, copy, place in ((has_up, nexts[1], 0), (has_dn, nexts[2], tall + 1)):
                @pl.when(cond)
                def _():
                    copy.wait_recv()
                    activate_block(buf, coef, 0, LEAD, place, 1)

        @pl.when(jnp.logical_not(has_prev))
        def _():
            for f in range(LEAD):
                act[f] = act[LEAD]

    def forward_edges(ups, dns, ups_more, dns_more, nexts):
        for cond, copies, more, copy in (
            (has_up, dns, dns_more, nexts[1]), (has_dn, ups, ups_more, nexts[2])
        ):
            @pl.when(cond)
            def _():
                copies[0].wait_recv()
                if more:
                    more[0].wait_recv()
                when(has_next, copy.start)

    def conv(frame, group, big, bias):
        cells = lambda i: act[frame + i, own_cols, group * rows * span : (group * rows + rows + 2) * span]
        summed = jnp.dot(cells(0), big[0], preferred_element_type=jnp.float32)
        for i in range(1, 3):
            summed = summed + jnp.dot(cells(i), big[i], preferred_element_type=jnp.float32)
        return [summed[:, o * chans : (o + 1) * chans] + bias for o in range(rows)]

    load_x.wait()
    part = summed_part(frames * rows, lambda n: x_ref[n // rows, n % rows])
    pl.semaphore_wait(barrier, row_count + tm_count - 2)
    copies_a1 = stats_rows(0, part)
    for copy in swap:
        copy.start()
    load_raw.wait()
    for p in range(2):
        when(jnp.logical_and(left_side, has_up), ups1[p].start)
        when(jnp.logical_and(side == 1, has_dn), dns1[p].start)

    for big in (big1, big2):
        for i in range(3):
            for o in range(rows):
                cols = pl.ds(o * chans, chans)
                if o > 0:
                    big[i, pl.ds(0, o * span), cols] = jnp.zeros((o * span, chans), jnp.bfloat16)
                rest = (rows - 1 - o) * span
                if rest > 0:
                    big[i, pl.ds(o * span + depth, rest), cols] = jnp.zeros((rest, chans), jnp.bfloat16)

    for cond, place in ((has_up, 0), (has_dn, tall + 1)):
        @pl.when(jnp.logical_not(cond))
        def _():
            for f in range(frames + LEAD):
                act[f, :, pl.ds(place * span, span)] = jnp.zeros((window, span), jnp.bfloat16)

    for copy in load_small:
        copy.wait()
    copies_b1 = stats_tm(0, collect(0, copies_a1, stat_a))

    def forward_swapped(p):
        swap[p].wait_recv()
        when(jnp.logical_and(side == 1, has_up), ups1[p].start)
        when(jnp.logical_and(left_side, has_dn), dns1[p].start)

    forward_swapped(0)
    when(has_next, nexts1[0].start)
    coef = coefficients(collect(0, copies_b1, stat_b), small[0], small[1])
    for r in range(rows):
        activate_block(raw, coef, LEAD, frames, 1 + side * rows + r, 1)
    forward_swapped(1)
    forward_edges(ups1, dns1, [], [], nexts1)
    for r in range(rows):
        activate_block(raw, coef, LEAD, frames, 1 + (1 - side) * rows + r, 1)
    for p in range(2):
        activate_edges(raw, coef, ups1, dns1, [], [], nexts1, p)
    activate_lead(raw, coef, nexts1)
    for copy in loads1:
        copy.wait()

    def first_conv(f):
        for g in range(2):
            for r, value in enumerate(conv(f, g, big1, small[2])):
                hid[f + LEAD, 1 + g * rows + r, own_cols] = value.astype(jnp.bfloat16)

    for p, (first, count) in enumerate(((early, late), (0, early))):
        @pl.loop(first, first + count)
        def _(f):
            first_conv(f)

        across[p].start()
        for cond, copies in ((has_up, (ups2, ups_across)), (has_dn, (dns2, dns_across))):
            for c in copies:
                when(cond, c[p].start)

    part = summed_part(
        frames * tall, lambda n: hid[LEAD + n // tall, 1 + n % tall, own_cols]
    )
    copies_a2 = stats_rows(1, part)
    across[0].wait_recv()
    when(has_next, nexts2[0].start)
    forward_edges(ups2, dns2, ups_across, dns_across, nexts2)
    copies_b2 = stats_tm(1, collect(1, copies_a2, stat_a))
    coef = coefficients(collect(1, copies_b2, stat_b), small[3], small[4])
    across[1].wait_recv()
    activate_block(hid, coef, LEAD, frames, 1, tall)
    for p in range(2):
        activate_edges(hid, coef, ups2, dns2, ups_across, dns_across, nexts2, p)
    activate_lead(hid, coef, nexts2)
    for copy in loads2:
        copy.wait()

    for f in range(frames):
        for g in range(2):
            values = conv(f, g, big2, small[5])
            results = [
                (value + raw[f + LEAD, 1 + g * rows + r, own_cols].astype(jnp.float32)).astype(jnp.bfloat16)
                for r, value in enumerate(values)
            ]

            @pl.when(side == g)
            def _():
                for r, value in enumerate(results):
                    out_buf[f, r, half_cols] = value

            @pl.when(side != g)
            def _():
                for r, value in enumerate(results):
                    stage[f, r] = value

        gives[f].start()

    stores = [
        pltpu.make_async_copy(out_buf.at[f], out_hbm.at[f], store_sem.at[f]) for f in range(frames)
    ]
    for f in range(frames):
        gives[f].wait_recv()
        stores[f].start()

    for copy in copies_a1 + copies_b1 + copies_a2 + copies_b2 + swap + across + gives:
        copy.wait_send()
    for cond, copies in (
        (has_up, ups1 + ups2 + ups_across),
        (has_dn, dns1 + dns2 + dns_across),
        (has_next, [nexts1[0], nexts2[0]]),
        (jnp.logical_and(has_next, has_up), [nexts1[1], nexts2[1]]),
        (jnp.logical_and(has_next, has_dn), [nexts1[2], nexts2[2]]),
    ):
        @pl.when(cond)
        def _():
            for copy in copies:
                copy.wait_send()
    for copy in stores:
        copy.wait()


def body(tm_count, row_count, features, gain1, shift1, w1, bias1, gain2, shift2, w2, bias2):
    frames, rows, width, chans = features.shape
    window = width // 2 + 16
    tall = 2 * rows
    lanes = (tall + 2) * 3 * chans
    hbm = pl.BlockSpec(memory_space=pl.ANY)
    bf16, f32 = jnp.bfloat16, jnp.float32
    dma = pltpu.SemaphoreType.DMA
    remote = 2 + 7 + 7 + 6 + frames
    return pl.pallas_call(
        functools.partial(kernel, tm_count, row_count),
        out_shape=jax.ShapeDtypeStruct(features.shape, bf16),
        in_specs=[hbm] * 9,
        out_specs=hbm,
        scratch_shapes=[
            pltpu.VMEM((frames, rows, width, chans), bf16),
            pltpu.VMEM((frames + LEAD, tall + 2, window, chans), bf16),
            pltpu.VMEM((frames + LEAD, tall + 2, window, chans), bf16),
            pltpu.VMEM((frames + LEAD, window, lanes), bf16),
            pltpu.VMEM((3, (rows + 2) * 3 * chans, rows * chans), bf16),
            pltpu.VMEM((3, (rows + 2) * 3 * chans, rows * chans), bf16),
            pltpu.VMEM((frames, rows, width // 2, chans), bf16),
            pltpu.VMEM((frames, rows, width, chans), bf16),
            pltpu.VMEM((6, 1, chans), f32),
            pltpu.VMEM((2, row_count, STAT_ROWS, chans), f32),
            pltpu.VMEM((2, tm_count, STAT_ROWS, chans), f32),
            dma((8,)),
            dma((2, 3 * rows)),
            dma((remote,)),
            dma((remote,)),
            dma((2, row_count)),
            dma((2, row_count)),
            dma((2, tm_count)),
            dma((2, tm_count)),
            dma((frames,)),
        ],
        compiler_params=pltpu.CompilerParams(
            collective_id=0, has_side_effects=True, vmem_limit_bytes=40 * 1024 * 1024
        ),
        name="block",
    )(
        features, gain1.reshape(1, -1), shift1.reshape(1, -1), w1, bias1.reshape(1, -1),
        gain2.reshape(1, -1), shift2.reshape(1, -1), w2, bias2.reshape(1, -1),
    )


def solution(mesh):
    in_specs = (P("tm", "rows", None, None), P(), P(), P(), P(), P(), P(), P(), P())
    out_specs = P("tm", "rows", None, None)
    return jax.shard_map(
        functools.partial(body, mesh.shape["tm"], mesh.shape["rows"]),
        mesh=mesh, in_specs=in_specs, out_specs=out_specs, check_vma=False,
    )
```

```python
import functools

import jax
import jax.numpy as jnp
from jax import lax
from jax.experimental import pallas as pl
from jax.experimental.pallas import tpu as pltpu
from jax.sharding import PartitionSpec as P

GROUPS = 32
EPS = 1e-06
LEAD = 2
STAT_ROWS = 8


def group_total(values, size):
    lanes = values.shape[-1]
    lane = lax.broadcasted_iota(jnp.int32, values.shape, 1)
    step = 1
    while step < size:
        left = pltpu.roll(values, step, 1)
        right = pltpu.roll(values, lanes - step, 1)
        values = values + jnp.where((lane & step) == 0, right, left)
        step *= 2
    return values


def kernel(
    tm_count, row_count,
    x_hbm, gain1_hbm, shift1_hbm, w1_ref, bias1_hbm, gain2_hbm, shift2_hbm, w2_ref, bias2_hbm,
    out_hbm,
    x_ref, raw, hid, act, big1, big2, stage, out_buf, small, stat_a, stat_b,
    load_sem, w_sem, send_sem, recv_sem, sa_send, sa_recv, sb_send, sb_recv, store_sem,
):
    frames, rows, width, chans = x_ref.shape
    window = raw.shape[2]
    half = width // 2
    pad = window - half
    tall = 2 * rows
    early, late = frames - LEAD, LEAD
    tm = lax.axis_index("tm")
    row = lax.axis_index("rows")
    side = lax.rem(row, 2)
    pair = row // 2
    partner = {"rows": row + 1 - 2 * side}
    has_up = pair > 0
    has_dn = pair < row_count // 2 - 1
    has_prev = tm > 0
    has_next = tm < tm_count - 1
    left_side = side == 0
    above_row = jnp.maximum(row - 2, side)
    below_row = jnp.minimum(row + 2, row_count - 2 + side)
    above, below = {"rows": above_row}, {"rows": below_row}
    above_across = {"rows": above_row + 1 - 2 * side}
    below_across = {"rows": below_row + 1 - 2 * side}
    after = {"tm": jnp.minimum(tm + 1, tm_count - 1)}
    span = 3 * chans
    depth = 3 * span
    size = chans // GROUPS
    total = float(frames * rows * width * size * tm_count * row_count)

    def aligned(value):
        return pl.multiple_of(value, 16)

    mine = pl.ds(aligned(side * (half - pad)), window)
    theirs = pl.ds(aligned((1 - side) * (half - pad)), window)
    own_rows = pl.ds(1 + side * rows, rows)
    own_cols = pl.ds(aligned(side * pad), half)
    edge_src = pl.ds(aligned(half - pad - side * (half - 2 * pad)), pad)
    edge_dst = pl.ds(aligned(side * half), pad)
    half_cols = pl.ds(aligned(side * half), half)

    def weight_copies(which, src, dst):
        return [
            pltpu.make_async_copy(
                src.at[pl.ds(i * depth, depth)],
                dst.at[i, pl.ds(o * span, depth), pl.ds(o * chans, chans)],
                w_sem.at[which, i * rows + o],
            )
            for i in range(3)
            for o in range(rows)
        ]

    load_x = pltpu.make_async_copy(x_hbm, x_ref, load_sem.at[0])
    load_raw = pltpu.make_async_copy(
        x_hbm.at[:, :, mine], raw.at[pl.ds(LEAD, frames), own_rows], load_sem.at[1]
    )
    load_small = [
        pltpu.make_async_copy(src, small.at[n], load_sem.at[2 + n])
        for n, src in enumerate((gain1_hbm, shift1_hbm, bias1_hbm, gain2_hbm, shift2_hbm, bias2_hbm))
    ]
    loads1 = weight_copies(0, w1_ref, big1)
    loads2 = weight_copies(1, w2_ref, big2)
    for copy in [load_x, load_raw] + load_small + loads1 + loads2:
        copy.start()

    barrier = pltpu.get_barrier_semaphore()
    for k in range(1, row_count):
        pl.semaphore_signal(barrier, inc=1, device_id={"rows": lax.rem(row + k, row_count)})
    for k in range(1, tm_count):
        pl.semaphore_signal(barrier, inc=1, device_id={"tm": lax.rem(tm + k, tm_count)})

    used = [0]

    def remote(source, target, device):
        n = used[0]
        used[0] += 1
        return pltpu.make_async_remote_copy(
            src_ref=source, dst_ref=target, send_sem=send_sem.at[n], recv_sem=recv_sem.at[n],
            device_id=device,
        )

    parts = (pl.ds(LEAD + early, late), pl.ds(LEAD, early))
    source_parts = (pl.ds(early, late), pl.ds(0, early))

    swap = [
        remote(x_hbm.at[s, :, theirs], raw.at[d, own_rows], partner)
        for s, d in zip(source_parts, parts)
    ]

    def halo_copies(buf, cols):
        ups = [remote(buf.at[d, 1, cols], buf.at[d, tall + 1, cols], above) for d in parts]
        dns = [remote(buf.at[d, tall, cols], buf.at[d, 0, cols], below) for d in parts]
        first = pl.ds(0, LEAD)
        nexts = [
            remote(buf.at[parts[0], r], buf.at[first, r], after)
            for r in (pl.ds(1, tall), 0, tall + 1)
        ]
        return ups, dns, nexts

    ups1, dns1, nexts1 = halo_copies(raw, pl.ds(0, window))
    ups2, dns2, nexts2 = halo_copies(hid, own_cols)
    across = [
        remote(hid.at[d, pl.ds(1, tall), edge_src], hid.at[d, pl.ds(1, tall), edge_dst], partner)
        for d in parts
    ]
    ups_across = [
        remote(hid.at[d, 1, edge_src], hid.at[d, tall + 1, edge_dst], above_across) for d in parts
    ]
    dns_across = [
        remote(hid.at[d, tall, edge_src], hid.at[d, 0, edge_dst], below_across) for d in parts
    ]
    gives = [
        remote(stage.at[f], out_buf.at[f, :, half_cols], partner) for f in range(frames)
    ]

    def when(cond, fn):
        pl.when(cond)(fn)

    def local_stats(cells):
        def add(n, carry):
            s, q = carry
            v = cells(n).astype(jnp.float32)
            v = v.reshape(v.shape[0] // 8, 8, chans)
            return s + jnp.sum(v, axis=0), q + jnp.sum(v * v, axis=0)

        zero = jnp.zeros((8, chans), jnp.float32)
        return zero, add

    def summed_part(count, cells):
        zero, add = local_stats(cells)
        first, square = lax.fori_loop(0, count, add, (zero, zero))
        return jnp.concatenate(
            [
                jnp.sum(first, axis=0, keepdims=True),
                jnp.sum(square, axis=0, keepdims=True),
                jnp.zeros((STAT_ROWS - 2, chans), jnp.float32),
            ],
            axis=0,
        )

    def send_stats(phase, part, axis, me, count, slots, send, recv):
        slots[phase, 0] = part
        copies = []
        for k in range(1, count):
            copy = pltpu.make_async_remote_copy(
                src_ref=slots.at[phase, 0], dst_ref=slots.at[phase, k],
                send_sem=send.at[phase, k], recv_sem=recv.at[phase, k],
                device_id={axis: lax.rem(me + k, count)},
            )
            copy.start()
            copies.append(copy)
        return copies

    def stats_rows(phase, part):
        return send_stats(phase, part, "rows", row, row_count, stat_a, sa_send, sa_recv)

    def stats_tm(phase, part):
        return send_stats(phase, part, "tm", tm, tm_count, stat_b, sb_send, sb_recv)

    def collect(phase, copies, slots):
        for copy in copies:
            copy.wait_recv()
        return jnp.sum(slots[phase], axis=0)

    def coefficients(part, gain, shift):
        mean = group_total(part, size) / total
        average = mean[0:1]
        spread = mean[1:2] - average * average
        return average, lax.rsqrt(spread + EPS) * gain * 0.5, shift * 0.5

    edge = lax.broadcasted_iota(jnp.int32, (window, chans), 0)

    def activate(cell, coef, frame, place):
        average, factor, offset = coef
        h = (cell.astype(jnp.float32) - average) * factor + offset
        value = h + h * jnp.tanh(h)
        left = jnp.where(edge == 0, 0.0, pltpu.roll(value, 1, 0))
        right = jnp.where(edge == window - 1, 0.0, pltpu.roll(value, window - 1, 0))
        base = pl.multiple_of(place * span, chans)
        act[frame, :, pl.ds(base, chans)] = left.astype(jnp.bfloat16)
        act[frame, :, pl.ds(base + chans, chans)] = value.astype(jnp.bfloat16)
        act[frame, :, pl.ds(base + 2 * chans, chans)] = right.astype(jnp.bfloat16)

    def activate_block(buf, coef, first, count, top, height):
        @pl.loop(0, count * height)
        def _(n):
            f, r = first + n // height, top + n % height
            activate(buf[f, r], coef, f, r)

    def activate_edges(buf, coef, ups, dns, ups_more, dns_more, nexts, part):
        first, count = ((LEAD + early, late), (LEAD, early))[part]
        for cond, copies, more, place in (
            (has_up, dns, dns_more, 0), (has_dn, ups, ups_more, tall + 1)
        ):
            @pl.when(cond)
            def _():
                if part == 1:
                    copies[part].wait_recv()
                    if more:
                        more[part].wait_recv()
                activate_block(buf, coef, first, count, place, 1)

    def activate_lead(buf, coef, nexts):
        @pl.when(has_prev)
        def _():
            nexts[0].wait_recv()
            activate_block(buf, coef, 0, LEAD, 1, tall)
            for cond, copy, place in ((has_up, nexts[1], 0), (has_dn, nexts[2], tall + 1)):
                @pl.when(cond)
                def _():
                    copy.wait_recv()
                    activate_block(buf, coef, 0, LEAD, place, 1)

        @pl.when(jnp.logical_not(has_prev))
        def _():
            for f in range(LEAD):
                act[f] = act[LEAD]

    def forward_edges(ups, dns, ups_more, dns_more, nexts):
        for cond, copies, more, copy in (
            (has_up, dns, dns_more, nexts[1]), (has_dn, ups, ups_more, nexts[2])
        ):
            @pl.when(cond)
            def _():
                copies[0].wait_recv()
                if more:
                    more[0].wait_recv()
                when(has_next, copy.start)

    def conv(frame, count, group, big, bias):
        lanes = slice(group * rows * span, (group * rows + rows + 2) * span)
        cells = lambda i: act[pl.ds(frame + i, count), own_cols, lanes].reshape(count * half, -1)
        summed = jnp.dot(cells(0), big[0], preferred_element_type=jnp.float32)
        for i in range(1, 3):
            summed = summed + jnp.dot(cells(i), big[i], preferred_element_type=jnp.float32)
        return [
            (summed[:, o * chans : (o + 1) * chans] + bias).reshape(count, half, chans)
            for o in range(rows)
        ]

    load_x.wait()
    part = summed_part(frames * rows, lambda n: x_ref[n // rows, n % rows])
    pl.semaphore_wait(barrier, row_count + tm_count - 2)
    copies_a1 = stats_rows(0, part)
    for copy in swap:
        copy.start()
    load_raw.wait()
    for p in range(2):
        when(jnp.logical_and(left_side, has_up), ups1[p].start)
        when(jnp.logical_and(side == 1, has_dn), dns1[p].start)

    for big in (big1, big2):
        for i in range(3):
            for o in range(rows):
                cols = pl.ds(o * chans, chans)
                if o > 0:
                    big[i, pl.ds(0, o * span), cols] = jnp.zeros((o * span, chans), jnp.bfloat16)
                rest = (rows - 1 - o) * span
                if rest > 0:
                    big[i, pl.ds(o * span + depth, rest), cols] = jnp.zeros((rest, chans), jnp.bfloat16)

    for cond, place in ((has_up, 0), (has_dn, tall + 1)):
        @pl.when(jnp.logical_not(cond))
        def _():
            for f in range(frames + LEAD):
                act[f, :, pl.ds(place * span, span)] = jnp.zeros((window, span), jnp.bfloat16)

    for copy in load_small:
        copy.wait()
    copies_b1 = stats_tm(0, collect(0, copies_a1, stat_a))

    def forward_swapped(p):
        swap[p].wait_recv()
        when(jnp.logical_and(side == 1, has_up), ups1[p].start)
        when(jnp.logical_and(left_side, has_dn), dns1[p].start)

    forward_swapped(0)
    when(has_next, nexts1[0].start)
    coef = coefficients(collect(0, copies_b1, stat_b), small[0], small[1])
    for r in range(rows):
        activate_block(raw, coef, LEAD, frames, 1 + side * rows + r, 1)
    forward_swapped(1)
    forward_edges(ups1, dns1, [], [], nexts1)
    for r in range(rows):
        activate_block(raw, coef, LEAD, frames, 1 + (1 - side) * rows + r, 1)
    for p in range(2):
        activate_edges(raw, coef, ups1, dns1, [], [], nexts1, p)
    activate_lead(raw, coef, nexts1)
    for copy in loads1:
        copy.wait()

    for p, (first, count) in enumerate(((early, late), (0, early))):
        for g in range(2):
            for r, value in enumerate(conv(first, count, g, big1, small[2])):
                hid[parts[p], 1 + g * rows + r, own_cols] = value.astype(jnp.bfloat16)

        across[p].start()
        for cond, copies in ((has_up, (ups2, ups_across)), (has_dn, (dns2, dns_across))):
            for c in copies:
                when(cond, c[p].start)

    part = summed_part(
        frames * tall, lambda n: hid[LEAD + n // tall, 1 + n % tall, own_cols]
    )
    copies_a2 = stats_rows(1, part)
    across[0].wait_recv()
    when(has_next, nexts2[0].start)
    forward_edges(ups2, dns2, ups_across, dns_across, nexts2)
    copies_b2 = stats_tm(1, collect(1, copies_a2, stat_a))
    coef = coefficients(collect(1, copies_b2, stat_b), small[3], small[4])
    across[1].wait_recv()
    activate_block(hid, coef, LEAD, frames, 1, tall)
    for p in range(2):
        activate_edges(hid, coef, ups2, dns2, ups_across, dns_across, nexts2, p)
    activate_lead(hid, coef, nexts2)
    for copy in loads2:
        copy.wait()

    for first, count in ((0, early), (early, late)):
        block = pl.ds(first, count)
        for g in range(2):
            values = conv(first, count, g, big2, small[5])
            results = [
                (value + raw[pl.ds(first + LEAD, count), 1 + g * rows + r, own_cols].astype(jnp.float32)).astype(jnp.bfloat16)
                for r, value in enumerate(values)
            ]

            @pl.when(side == g)
            def _():
                for r, value in enumerate(results):
                    out_buf[block, r, half_cols] = value

            @pl.when(side != g)
            def _():
                for r, value in enumerate(results):
                    stage[block, r] = value

        for f in range(first, first + count):
            gives[f].start()

    stores = [
        pltpu.make_async_copy(out_buf.at[f], out_hbm.at[f], store_sem.at[f]) for f in range(frames)
    ]
    for f in range(frames):
        gives[f].wait_recv()
        stores[f].start()

    for copy in copies_a1 + copies_b1 + copies_a2 + copies_b2 + swap + across + gives:
        copy.wait_send()
    for cond, copies in (
        (has_up, ups1 + ups2 + ups_across),
        (has_dn, dns1 + dns2 + dns_across),
        (has_next, [nexts1[0], nexts2[0]]),
        (jnp.logical_and(has_next, has_up), [nexts1[1], nexts2[1]]),
        (jnp.logical_and(has_next, has_dn), [nexts1[2], nexts2[2]]),
    ):
        @pl.when(cond)
        def _():
            for copy in copies:
                copy.wait_send()
    for copy in stores:
        copy.wait()


def body(tm_count, row_count, features, gain1, shift1, w1, bias1, gain2, shift2, w2, bias2):
    frames, rows, width, chans = features.shape
    window = width // 2 + 16
    tall = 2 * rows
    lanes = (tall + 2) * 3 * chans
    hbm = pl.BlockSpec(memory_space=pltpu.HBM)
    bf16, f32 = jnp.bfloat16, jnp.float32
    dma = pltpu.SemaphoreType.DMA
    remote = 2 + 7 + 7 + 6 + frames
    return pl.pallas_call(
        functools.partial(kernel, tm_count, row_count),
        out_shape=jax.ShapeDtypeStruct(features.shape, bf16),
        in_specs=[hbm] * 9,
        out_specs=hbm,
        scratch_shapes=[
            pltpu.VMEM((frames, rows, width, chans), bf16),
            pltpu.VMEM((frames + LEAD, tall + 2, window, chans), bf16),
            pltpu.VMEM((frames + LEAD, tall + 2, window, chans), bf16),
            pltpu.VMEM((frames + LEAD, window, lanes), bf16),
            pltpu.VMEM((3, (rows + 2) * 3 * chans, rows * chans), bf16),
            pltpu.VMEM((3, (rows + 2) * 3 * chans, rows * chans), bf16),
            pltpu.VMEM((frames, rows, width // 2, chans), bf16),
            pltpu.VMEM((frames, rows, width, chans), bf16),
            pltpu.VMEM((6, 1, chans), f32),
            pltpu.VMEM((2, row_count, STAT_ROWS, chans), f32),
            pltpu.VMEM((2, tm_count, STAT_ROWS, chans), f32),
            dma((8,)),
            dma((2, 3 * rows)),
            dma((remote,)),
            dma((remote,)),
            dma((2, row_count)),
            dma((2, row_count)),
            dma((2, tm_count)),
            dma((2, tm_count)),
            dma((frames,)),
        ],
        compiler_params=pltpu.CompilerParams(
            collective_id=0, has_side_effects=True, vmem_limit_bytes=65000 * 1024
        ),
        name="block",
    )(
        features, gain1.reshape(1, -1), shift1.reshape(1, -1), w1, bias1.reshape(1, -1),
        gain2.reshape(1, -1), shift2.reshape(1, -1), w2, bias2.reshape(1, -1),
    )


def solution(mesh):
    in_specs = (P("tm", "rows", None, None), P(), P(), P(), P(), P(), P(), P(), P())
    out_specs = P("tm", "rows", None, None)
    return jax.shard_map(
        functools.partial(body, mesh.shape["tm"], mesh.shape["rows"]),
        mesh=mesh, in_specs=in_specs, out_specs=out_specs, check_vma=False,
    )
```
